128 devices in a mesh: space: 8 (over y, core), energy: 16 (over z, x).
Axes of the slice: x: 4, y: 4, z: 4, core: 2. Of those that a mesh axis runs over, the one named last changes fastest.
Arguments:
- ham_diag: float32 [16, 2, 128, 128], P('space'), may hold values from -0.5 to 0.5
- coupling: float32 [16, 2, 128, 128], P('space'), may hold values from -0.5 to 0.5
- contact_left: float32 [2, 128, 128], replicated, may hold values from -0.5 to 0.5
- mode_weight: float32 [4], replicated, may hold values from 0.5 to 2
- mode_offset: int32 [4], replicated, may hold values from -8 to 8, as said below
- pattern: int32 [128, 128], replicated, may hold values 0 or 1
Outputs:
- sigma: float32 [16, 16, 2, 128, 128], P('energy', 'space')
The draws below stay inside these ranges and needn't reach their ends.
Inputs may be any that keep to these rules, and one draw needn't show every extreme that they name: `mode_offset`: the offsets are -1, 1, -8 and 8 in some order.
All inputs are finite; a program needn't handle non-finite values.
Results may differ from the reference program's by a relative error of at most 0.0003.
Values sent between devices are 32-bit elements; how exact they have to be, the bound alone decides.
A program may use at most 64 MiB of HBM per device.

```python
import math
import jax
import jax.numpy as jnp
from jax import lax

B = 128
MODES = 4
NB = 16
ENERGIES = 16


def draw_mode_offset(key, part):
    half_grid = ENERGIES // 2
    offsets = jnp.array([-1, 1, 0 - half_grid, half_grid], dtype=jnp.int32)
    order = jax.random.permutation(jax.random.fold_in(key, 7), MODES)
    return offsets[order].astype(jnp.int32)


def with_ends(values, key, least, top_value):
    extent = values.shape
    spot = [jax.random.randint(jax.random.fold_in(key, axis), (), 0, extent[axis]) for axis in range(len(extent))]
    values = values.at[tuple(spot)].set(least)
    longest = extent.index(max(extent))
    spot[longest] = (spot[longest] + 1) % extent[longest]
    return values.at[tuple(spot)].set(top_value)


def levels(rng, extent, split, low, high):
    def one(position, shards_of):
        heights = jax.random.uniform(jax.random.fold_in(jax.random.fold_in(rng, 6), position), (shards_of,), jnp.float32, low / len(split), high / len(split))
        return jnp.repeat(jnp.exp(heights), extent[position] // shards_of).reshape((-1,) + (1,) * (len(extent) - position - 1))

    level = one(*split[0])
    for cut in split[1:]:
        level = level * one(*cut)
    return level


def bell_draw(own_key, dims, spread, most, cuts=(), held_as=jnp.bfloat16):
    result = spread * jax.random.normal(own_key, dims, jnp.float32)
    if cuts:
        result = result * levels(own_key, dims, cuts, -0.22, 0.18)
    return jnp.clip(result, -most, most).astype(held_as)


def setup_inputs(seed: int = 0) -> dict:
    key_list = jax.random.split(jax.random.key(seed), 7)
    ham_diag = bell_draw(key_list[0], (NB, 2, B, B), B ** -0.5, 0.5, ((0, 8),), jnp.float32)
    coupling = bell_draw(key_list[1], (NB, 2, B, B), B ** -0.5, 0.5, ((0, 8),), jnp.float32)
    contact_left = bell_draw(key_list[2], (2, B, B), B ** -0.5, 0.5, (), jnp.float32)
    mode_weight = jnp.clip(jnp.exp(jax.random.uniform(key_list[3], (MODES,), jnp.float32, math.log(0.5), math.log(2.0))), 0.5, 2.0)
    mode_offset = draw_mode_offset(jax.random.fold_in(key_list[6], 71), 0)
    pattern = with_ends((jax.random.randint(key_list[5], (B, B), 0, 2) < 1).astype(jnp.int32), jax.random.fold_in(key_list[5], 1), 0, 1)
    return {"ham_diag": ham_diag, "coupling": coupling, "contact_left": contact_left, "mode_weight": mode_weight, "mode_offset": mode_offset, "pattern": pattern}


HIGHEST = lax.Precision.HIGHEST
BROADENING = 0.1

def product(former, latter):
    real_part = jnp.dot(former[0], latter[0], precision=HIGHEST) - jnp.dot(former[1], latter[1], precision=HIGHEST)
    imag_part = jnp.dot(former[0], latter[1], precision=HIGHEST) + jnp.dot(former[1], latter[0], precision=HIGHEST)
    return jnp.stack([real_part, imag_part])

def adjoint(matrix):
    return jnp.stack([matrix[0].T, -matrix[1].T])

def times_imag(matrix):
    return jnp.stack([-matrix[1], matrix[0]])

def hermitian(matrix):
    return 0.5 * (matrix + adjoint(matrix))

def unit_block(order_size):
    identity_real = jnp.eye(order_size, dtype=jnp.float32)
    return jnp.stack([identity_real, jnp.zeros_like(identity_real)])

def invert(matrix):
    order_size = matrix.shape[1]
    real_form = jnp.concatenate([jnp.concatenate([matrix[0], -matrix[1]], 1), jnp.concatenate([matrix[1], matrix[0]], 1)], 0)
    inverse_form = jnp.linalg.inv(real_form)
    return jnp.stack([inverse_form[:order_size, :order_size], inverse_form[order_size:, :order_size]])

def green_diagonal(blocks, links):

    def forward_step(previous, element):
        diag_block, bridge = element
        sigma_link = product(adjoint(bridge), product(previous, bridge))
        return (invert(diag_block - sigma_link), sigma_link)
    sigma_before = lax.scan(forward_step, invert(blocks[0]), (blocks[1:], links))[1]

    def backward_step(following, element):
        diag_block, bridge = element
        sigma_link = product(bridge, product(following, adjoint(bridge)))
        return (invert(diag_block - sigma_link), sigma_link)
    sigma_after = lax.scan(backward_step, invert(blocks[-1]), (blocks[:-1], links), reverse=True)[1]
    padding = jnp.zeros_like(blocks[:1])
    sigma_before = jnp.concatenate([padding, sigma_before], 0)
    sigma_after = jnp.concatenate([sigma_after, padding], 0)
    return jax.vmap(invert)(blocks - sigma_before - sigma_after)

def mode_table(targets, sources, mode_weight, mode_offset):
    hits = (sources[None, :, None] == targets[:, None, None] - mode_offset[None, None, :]).astype(jnp.float32)
    return jnp.sum(hits * mode_weight[None, None, :], axis=2)

def reference(ham_diag, coupling, contact_left, mode_weight, mode_offset, pattern):
    order_size = ham_diag.shape[-1]
    unit = unit_block(order_size)
    onsite = -jax.vmap(hermitian)(ham_diag)
    onsite = onsite.at[0].add(times_imag(0.5 * product(contact_left, adjoint(contact_left))))
    onsite = onsite.at[-1].add(times_imag(0.5 * product(adjoint(coupling[-1]), coupling[-1])))
    links = coupling[:-1]
    energy_grid = jnp.arange(ENERGIES, dtype=jnp.int32)
    energies = -2.0 + 4.0 * (energy_grid.astype(jnp.float32) + 0.5) / ENERGIES

    def solve_energy(energy):
        shift = energy * unit + BROADENING * times_imag(unit)
        return green_diagonal(onsite + shift[None], links)
    green = lax.map(solve_energy, energies)
    table = mode_table(energy_grid, energy_grid, mode_weight, mode_offset)
    sigma = jnp.einsum('ef,fkxab->ekxab', table, green, precision=HIGHEST)
    return sigma * pattern.astype(jnp.float32)
```

```python
import functools

import jax
import jax.numpy as jnp
from jax import lax
from jax.experimental import pallas as pl
from jax.experimental.pallas import tpu as pltpu
from jax.sharding import PartitionSpec as P

N = 128
PANEL = 16
ENERGIES = 16
BROADENING = 0.1
F32 = jnp.float32
MESH = pl.DeviceIdType.MESH
VM = pl.BlockSpec(memory_space=pltpu.VMEM)
HIGHEST = lax.Precision.HIGHEST
BLOCK = (2, N, N)


def split(x):
    high = x.astype(jnp.bfloat16)
    return high, (x - high.astype(F32)).astype(jnp.bfloat16)


def dot3(a, b):
    ah, al = split(a)
    bh, bl = split(b)
    d = functools.partial(jnp.dot, preferred_element_type=F32)
    return d(ah, bh) + (d(al, bh) + d(ah, bl))


def dot6(a, b):
    return jnp.dot(a, b, precision=HIGHEST, preferred_element_type=F32)


def mul(a, b, dot=dot6):
    left = jnp.concatenate([a[0], a[1]], 1)
    right = jnp.concatenate(
        [jnp.concatenate([b[0], b[1]], 1), jnp.concatenate([-b[1], b[0]], 1)], 0
    )
    out = dot(left, right)
    return out[:, :N], out[:, N:]


def add(a, b):
    return a[0] + b[0], a[1] + b[1]


def sub(a, b):
    return a[0] - b[0], a[1] - b[1]


def adj(a):
    return a[0].T, -a[1].T


def pick(cond, a, b):
    return jnp.where(cond, a[0], b[0]), jnp.where(cond, a[1], b[1])


def get(ref, *index):
    return ref[index + (0,)], ref[index + (1,)]


def put(ref, value, *index):
    ref[index + (0,)] = value[0]
    ref[index + (1,)] = value[1]


def rows8(x):
    return jnp.broadcast_to(x, (8, N))


def eliminate8(rr, ri, dr, di, g):
    row = lax.broadcasted_iota(jnp.int32, (8, N), 0)
    groups = len(rr)
    for k in range(8):
        pr, pi = rows8(dr[k][g][k : k + 1]), rows8(di[k][g][k : k + 1])
        inv = 1.0 / (pr * pr + pi * pi)
        qr, qi = pr * inv, -pi * inv
        at_pivot = row == k

        def step(xr, xi):
            ar, ai = rows8(xr[g][k : k + 1]), rows8(xi[g][k : k + 1])
            sr, si = qr * ar - qi * ai, qr * ai + qi * ar
            outr, outi = [], []
            for v in range(groups):
                yr = xr[v] - dr[k][v] * sr + di[k][v] * si
                yi = xi[v] - dr[k][v] * si - di[k][v] * sr
                if v == g:
                    yr, yi = jnp.where(at_pivot, sr, yr), jnp.where(at_pivot, si, yi)
                outr.append(yr)
                outi.append(yi)
            return outr, outi

        for j in range(k + 1, 8):
            dr[j], di[j] = step(dr[j], di[j])
        rr, ri = step(rr, ri)
    return rr, ri


def invert(ref):
    groups = PANEL // 8
    lane8 = lax.broadcasted_iota(jnp.int32, (8, N), 1)
    row8 = lax.broadcasted_iota(jnp.int32, (8, N), 0)
    lane = lax.broadcasted_iota(jnp.int32, (N, N), 1)
    for first in range(0, N, PANEL):
        span = [pl.ds(first + 8 * v, 8) for v in range(groups)]
        rr = [ref[0, s, :] for s in span]
        ri = [ref[1, s, :] for s in span]
        for g in range(groups):
            c0 = first + 8 * g
            dr = [[rows8_lane(rr[v], c0 + j) for v in range(groups)] for j in range(8)]
            di = [[rows8_lane(ri[v], c0 + j) for v in range(groups)] for j in range(8)]
            here = (lane8 >= c0) & (lane8 < c0 + 8)
            unit = jnp.where(lane8 - c0 == row8, 1.0, 0.0)
            rr = [jnp.where(here, unit if v == g else 0.0, rr[v]) for v in range(groups)]
            ri = [jnp.where(here, 0.0, ri[v]) for v in range(groups)]
            rr, ri = eliminate8(rr, ri, dr, di, g)
        pr, pi = jnp.concatenate(rr, 0), jnp.concatenate(ri, 0)

        def gap(rows):
            return [jnp.zeros((rows, 2 * N), F32)] if rows else []

        right = jnp.concatenate(
            gap(first)
            + [jnp.concatenate([pr, pi], 1)]
            + gap(N - PANEL)
            + [jnp.concatenate([-pi, pr], 1)]
            + gap(N - PANEL - first),
            0,
        )
        ar, ai = ref[0], ref[1]
        change = dot3(jnp.concatenate([ar, ai], 1), right)
        inside = (lane >= first) & (lane < first + PANEL)
        ref[0] = jnp.where(inside, 0.0, ar) - change[:, :N]
        ref[1] = jnp.where(inside, 0.0, ai) - change[:, N:]
        ref[0, first : first + PANEL, :] = pr
        ref[1, first : first + PANEL, :] = pi


def rows8_lane(x, lane):
    return jnp.broadcast_to(x[:, lane : lane + 1], (8, N))


def meet(partners):
    barrier = pltpu.get_barrier_semaphore()
    for partner in partners:
        pl.semaphore_signal(barrier, inc=1, device_id=partner, device_id_type=MESH)
    pl.semaphore_wait(barrier, len(partners))


def gather_kernel(ham, coupling, ham4, link5, local, send, recv):
    s, e = lax.axis_index("space"), lax.axis_index("energy")
    y, core = s // 2, s % 2
    nxt, prv = (y + 1) % 4, (y + 3) % 4
    other = (y * 2 + 1 - core, e)
    ahead = [(nxt * 2, e), (nxt * 2 + 1, e)]
    behind = [(prv * 2, e), (prv * 2 + 1, e)]
    meet([other] + ahead + behind)
    base = core * 2
    mine = [
        pltpu.make_async_copy(ham, ham4.at[pl.ds(base, 2)], local.at[0]),
        pltpu.make_async_copy(coupling, link5.at[pl.ds(base + 1, 2)], local.at[1]),
    ]

    def remote(src, dst, i, to):
        return pltpu.make_async_remote_copy(
            src, dst, send.at[i], recv.at[i], device_id=to, device_id_type=MESH
        )

    last = [remote(coupling.at[1], link5.at[0], i, ahead[i]) for i in range(2)]

    @pl.when(core == 1)
    def _():
        last[0].start()
        last[1].start()

    pair = [
        remote(ham, ham4.at[pl.ds(base, 2)], 2, other),
        remote(coupling, link5.at[pl.ds(base + 1, 2)], 3, other),
    ]
    for c in pair + mine:
        c.start()
    for c in pair + mine:
        c.wait()

    @pl.when(core == 1)
    def _():
        last[0].wait_send()
        last[1].wait_send()
        last[1].wait_recv()

    @pl.when(core == 0)
    def _():
        last[0].wait_recv()


def swap_kernel(partner_of, x, out, send, recv):
    s, e = lax.axis_index("space"), lax.axis_index("energy")
    partner = (partner_of(s // 2) * 2 + s % 2, e)
    meet([partner])
    copy = pltpu.make_async_remote_copy(
        x, out, send, recv, device_id=partner, device_id_type=MESH
    )
    copy.start()
    copy.wait()


def energy_kernel(x, out, send, recv):
    s, e = lax.axis_index("space"), lax.axis_index("energy")
    targets = [(s, (e + d) % ENERGIES) for d in (1, ENERGIES - 1, ENERGIES // 2)]
    meet(targets)
    copies = [
        pltpu.make_async_remote_copy(
            x, out.at[i], send.at[i], recv.at[i], device_id=to, device_id_type=MESH
        )
        for i, to in enumerate(targets)
    ]
    for c in copies:
        c.start()
    for c in copies:
        c.wait()


def swap(x, partner_of, identity):
    return pl.pallas_call(
        functools.partial(swap_kernel, partner_of),
        out_shape=jax.ShapeDtypeStruct(x.shape, F32),
        in_specs=[VM],
        out_specs=VM,
        scratch_shapes=[pltpu.SemaphoreType.DMA, pltpu.SemaphoreType.DMA],
        compiler_params=pltpu.CompilerParams(collective_id=identity, has_side_effects=True),
    )(x)


def across_pair(y):
    return y + 1 - 2 * (y % 2)


def across_middle(y):
    return 3 - y


def chain_kernel(ham4, link5, contact, state, parts, s_ref, a_ref, b_ref, h_ref, g_ref, p_ref, q_ref, ef_ref):
    space = lax.axis_index("space")
    y, core = space // 2, space % 2
    right = y >= 2
    outer = (y == 0) | (y == 3)
    inner_core = jnp.where(right, 1 - core, core) == 1
    energy = -2.0 + 4.0 * (lax.axis_index("energy").astype(F32) + 0.5) / ENERGIES
    eye = jnp.where(
        lax.broadcasted_iota(jnp.int32, (N, N), 0) == lax.broadcasted_iota(jnp.int32, (N, N), 1), 1.0, 0.0
    )

    def oriented(index):
        c = get(link5, index)
        return pick(right, adj(c), c)

    for k in range(4):
        h = get(ham4, jnp.where(right, 3 - k, k))
        a_ref[k, 0] = energy * eye - 0.5 * (h[0] + h[0].T)
        a_ref[k, 1] = BROADENING * eye - 0.5 * (h[1] - h[1].T)
    for k in range(3):
        b = oriented(jnp.where(right, 3 - k, k + 1))
        put(b_ref, b, k)
        put(h_ref, adj(b), k)
    ext = oriented(jnp.where(right, 4, 0))
    lead = pick(right, ext, get(contact))
    gamma = mul(lead, adj(lead))
    weight = jnp.where(outer, 0.5, 0.0)
    put(s_ref, (a_ref[0, 0] - weight * gamma[1], a_ref[0, 1] + weight * gamma[0]))
    zero = jnp.zeros((N, N), F32)
    ext = pick(outer, (zero, zero), ext)
    put(ef_ref, ext, 0, 0)
    put(ef_ref, adj(ext), 1, 0)
    put(state, (zero, zero), 3)

    def level(k, _):
        invert(s_ref)
        g = get(s_ref)
        put(g_ref, g, k)
        b, bh = get(b_ref, k), get(h_ref, k)
        p = mul(g, b)
        put(s_ref, sub(get(a_ref, k + 1), mul(bh, p)))
        q = mul(bh, g)
        put(p_ref, p, k)
        put(q_ref, q, k)
        e, f = get(ef_ref, 0, k), get(ef_ref, 1, k)
        put(ef_ref, mul(e, p), 0, k + 1)
        put(ef_ref, mul(q, f), 1, k + 1)
        put(state, add(get(state, 3), mul(mul(e, g), f)), 3)
        return 0

    lax.fori_loop(0, 3, level, 0)
    put(state, get(s_ref), 0)
    put(state, get(ef_ref, 0, 3), 1)
    put(state, get(ef_ref, 1, 3), 2)

    @pl.when(inner_core)
    def _():
        g2 = get(g_ref, 2)
        put(parts, g2, 0, 0)
        put(parts, get(p_ref, 2), 0, 1)
        put(parts, get(q_ref, 2), 0, 2)
        put(parts, mul(g2, get(ef_ref, 1, 2)), 0, 3)
        put(parts, mul(get(ef_ref, 0, 2), g2), 0, 4)
        put(parts, (zero, zero), 1, 0)
        put(parts, (eye, zero), 1, 1)
        put(parts, (eye, zero), 1, 2)
        put(parts, (zero, zero), 1, 3)
        put(parts, (zero, zero), 1, 4)

    @pl.when(jnp.logical_not(inner_core))
    def _():
        p0, p1, q0, q1 = get(p_ref, 0), get(p_ref, 1), get(q_ref, 0), get(q_ref, 1)
        w1 = add(get(g_ref, 1), mul(mul(p1, get(g_ref, 2)), q1))
        l1, r1 = mul(p1, get(p_ref, 2)), mul(get(q_ref, 2), q1)
        put(parts, w1, 0, 0)
        put(parts, l1, 0, 1)
        put(parts, r1, 0, 2)
        put(parts, mul(w1, get(ef_ref, 1, 1)), 0, 3)
        put(parts, mul(get(ef_ref, 0, 1), w1), 0, 4)
        w0 = add(get(g_ref, 0), mul(mul(p0, w1), q0))
        put(parts, w0, 1, 0)
        put(parts, mul(p0, l1), 1, 1)
        put(parts, mul(r1, q0), 1, 2)
        put(parts, mul(w0, get(ef_ref, 1, 0)), 1, 3)
        put(parts, mul(get(ef_ref, 0, 0), w0), 1, 4)


def outer_join_kernel(state, theirs, parts_in, schur, join, parts, s_ref):
    put(s_ref, sub(get(theirs), get(state, 3)))
    invert(s_ref)
    k = get(s_ref)
    e3, f3 = get(state, 1), get(state, 2)
    ke, fk = mul(k, e3), mul(f3, k)
    put(schur, sub(get(state, 0), mul(f3, ke)))
    put(join, k, 0)
    put(join, ke, 1)
    put(join, fk, 2)
    for t in range(2):
        le, re = get(parts_in, t, 3), get(parts_in, t, 4)
        put(parts, add(get(parts_in, t, 0), mul(mul(le, k), re)), t, 0)
        put(parts, add(get(parts_in, t, 1), mul(le, ke)), t, 1)
        put(parts, add(get(parts_in, t, 2), mul(fk, re)), t, 2)


def middle_kernel(schur, theirs, link5, join, green, s_ref):
    right = lax.axis_index("space") // 2 >= 2
    c = get(link5, jnp.where(right, 0, 4))
    b = pick(right, adj(c), c)
    s_ref[...] = theirs[...]

    def level(k, _):
        invert(s_ref)

        @pl.when(k == 0)
        def _():
            put(s_ref, sub(get(schur), mul(mul(b, get(s_ref)), adj(b))))

        return 0

    lax.fori_loop(0, 2, level, 0)
    g = get(s_ref)
    put(green, g, 0)
    put(green, add(get(join, 0), mul(get(join, 1), mul(g, get(join, 2)))), 1)


def close_kernel(green, theirs, parts, out):
    space = lax.axis_index("space")
    y, core = space // 2, space % 2
    outer = (y == 0) | (y == 3)
    right = y >= 2
    inner_core = jnp.where(right, 1 - core, core) == 1
    x = pick(outer, get(theirs), get(green, 0))
    for t in range(2):
        put(
            out,
            add(get(parts, t, 0), mul(mul(get(parts, t, 1), x), get(parts, t, 2))),
            jnp.where(jnp.where(right, inner_core, jnp.logical_not(inner_core)), 1 - t, t),
        )


def call(kernel, outs, scratch, *args):
    return pl.pallas_call(
        kernel,
        out_shape=[jax.ShapeDtypeStruct(o, F32) for o in outs],
        in_specs=[VM] * len(args),
        out_specs=[VM] * len(outs),
        scratch_shapes=[pltpu.VMEM(s, F32) for s in scratch],
        compiler_params=pltpu.CompilerParams(vmem_limit_bytes=48 << 20),
    )(*args)


def on_device(ham_diag, coupling, contact_left, mode_weight, mode_offset, pattern):
    ham4, link5 = pl.pallas_call(
        gather_kernel,
        out_shape=[jax.ShapeDtypeStruct((4,) + BLOCK, F32), jax.ShapeDtypeStruct((5,) + BLOCK, F32)],
        in_specs=[VM] * 2,
        out_specs=[VM] * 2,
        scratch_shapes=[
            pltpu.SemaphoreType.DMA((2,)),
            pltpu.SemaphoreType.DMA((4,)),
            pltpu.SemaphoreType.DMA((4,)),
        ],
        compiler_params=pltpu.CompilerParams(collective_id=0, has_side_effects=True),
    )(ham_diag, coupling)
    state, parts = call(
        chain_kernel,
        [(4,) + BLOCK, (2, 5) + BLOCK],
        [BLOCK, (4,) + BLOCK, (3,) + BLOCK, (3,) + BLOCK, (3,) + BLOCK, (3,) + BLOCK, (3,) + BLOCK, (2, 4) + BLOCK],
        ham4,
        link5,
        contact_left,
    )
    theirs = swap(state[0], across_pair, 1)
    schur, join, parts = call(
        outer_join_kernel, [BLOCK, (3,) + BLOCK, (2, 3) + BLOCK], [BLOCK], state, theirs, parts
    )
    theirs = swap(schur, across_middle, 2)
    (green,) = call(middle_kernel, [(2,) + BLOCK], [BLOCK], schur, theirs, link5, join)
    theirs = swap(green[1], across_pair, 3)
    (diag,) = call(close_kernel, [(2,) + BLOCK], [], green, theirs, parts)
    got = pl.pallas_call(
        energy_kernel,
        out_shape=jax.ShapeDtypeStruct((3, 2) + BLOCK, F32),
        in_specs=[VM],
        out_specs=VM,
        scratch_shapes=[pltpu.SemaphoreType.DMA((3,)), pltpu.SemaphoreType.DMA((3,))],
        compiler_params=pltpu.CompilerParams(collective_id=4, has_side_effects=True),
    )(diag)
    e = lax.axis_index("energy")
    source = jnp.stack([e - 1, e + 1, jnp.where(e >= ENERGIES // 2, e - ENERGIES // 2, e + ENERGIES // 2)])
    hits = (source[:, None] == e - mode_offset[None, :]) & ((source >= 0) & (source < ENERGIES))[:, None]
    weight = jnp.sum(jnp.where(hits, mode_weight[None, :], 0.0), 1)
    total = got[0] * weight[0] + got[1] * weight[1] + got[2] * weight[2]
    return (total * pattern.astype(F32))[None]


def solution(mesh):
    placed = (P("space", None, None, None), P("space", None, None, None), P(), P(), P(), P())
    return jax.shard_map(
        on_device,
        mesh=mesh,
        in_specs=placed,
        out_specs=P("energy", "space", None, None, None),
        check_vma=False,
    )
```

```python
import functools

import jax
import jax.numpy as jnp
from jax import lax
from jax.experimental import pallas as pl
from jax.experimental.pallas import tpu as pltpu
from jax.sharding import PartitionSpec as P

N = 128
PANEL = 16
ENERGIES = 16
BROADENING = 0.1
F32 = jnp.float32
MESH = pl.DeviceIdType.MESH
VM = pl.BlockSpec(memory_space=pltpu.VMEM)
SM = pl.BlockSpec(memory_space=pltpu.SMEM)
HIGHEST = lax.Precision.HIGHEST
BLOCK = (2, N, N)
STEPS = (1, ENERGIES - 1, ENERGIES // 2)


def split(x):
    high = x.astype(jnp.bfloat16)
    return high, (x - high.astype(F32)).astype(jnp.bfloat16)


def dot3(a, b):
    ah, al = split(a)
    bh, bl = split(b)
    d = functools.partial(jnp.dot, preferred_element_type=F32)
    return d(ah, bh) + (d(al, bh) + d(ah, bl))


def dot6(a, b):
    return jnp.dot(a, b, precision=HIGHEST, preferred_element_type=F32)


def mul(a, b, dot=dot6):
    left = jnp.concatenate([a[0], a[1]], 1)
    right = jnp.concatenate(
        [jnp.concatenate([b[0], b[1]], 1), jnp.concatenate([-b[1], b[0]], 1)], 0
    )
    out = dot(left, right)
    return out[:, :N], out[:, N:]


def add(a, b):
    return a[0] + b[0], a[1] + b[1]


def sub(a, b):
    return a[0] - b[0], a[1] - b[1]


def adj(a):
    return a[0].T, -a[1].T


def pick(cond, a, b):
    return jnp.where(cond, a[0], b[0]), jnp.where(cond, a[1], b[1])


def get(ref, *index):
    return ref[index + (0,)], ref[index + (1,)]


def put(ref, value, *index):
    ref[index + (0,)] = value[0]
    ref[index + (1,)] = value[1]


def spread(x, rows):
    return jnp.broadcast_to(x, (rows, N))


def eliminate(rr, ri, first):
    b, groups = PANEL, PANEL // 8
    lane = lax.broadcasted_iota(jnp.int32, (b, N), 1)
    row = lax.broadcasted_iota(jnp.int32, (b, N), 0)
    for g in range(groups):
        c0 = first + 8 * g
        here = (lane >= c0) & (lane < c0 + 8)
        unit = jnp.where(lane - first == row, 1.0, 0.0)
        xr = jnp.stack([spread(rr[:, c0 + j : c0 + j + 1], b) for j in range(8)] + [jnp.where(here, unit, rr)])
        xi = jnp.stack([spread(ri[:, c0 + j : c0 + j + 1], b) for j in range(8)] + [jnp.where(here, 0.0, ri)])
        for k in range(8):
            t = 8 * g + k
            dr, di = xr[0], xi[0]
            xr, xi = xr[1:], xi[1:]
            pr, pi = spread(dr[t : t + 1], 8), spread(di[t : t + 1], 8)
            inv = 1.0 / (pr * pr + pi * pi)
            qr, qi = (pr * inv)[None], (-pi * inv)[None]
            shape = (8 - k, 8, N)
            ar = jnp.broadcast_to(xr[:, t : t + 1, :], shape)
            ai = jnp.broadcast_to(xi[:, t : t + 1, :], shape)
            sr, si = qr * ar - qi * ai, qr * ai + qi * ar
            outr, outi = [], []
            for v in range(groups):
                s = slice(8 * v, 8 * v + 8)
                yr = xr[:, s] - dr[None, s] * sr + di[None, s] * si
                yi = xi[:, s] - dr[None, s] * si - di[None, s] * sr
                if v == g:
                    at_pivot = (row[:8] == k)[None]
                    yr, yi = jnp.where(at_pivot, sr, yr), jnp.where(at_pivot, si, yi)
                outr.append(yr)
                outi.append(yi)
            xr, xi = jnp.concatenate(outr, 1), jnp.concatenate(outi, 1)
        rr, ri = xr[0], xi[0]
    return rr, ri


def inverse(a):
    ar, ai = a
    b = PANEL
    lane = lax.broadcasted_iota(jnp.int32, (N, N), 1)
    d = functools.partial(jnp.dot, preferred_element_type=F32)
    ahead = (ar[:b], ai[:b])
    for f in range(0, N, b):
        pr, pi = eliminate(*ahead, f)
        inside = (lane >= f) & (lane < f + b)
        zr, zi = jnp.where(inside, 0.0, ar), jnp.where(inside, 0.0, ai)
        ahead = None
        n0 = f + b
        if n0 < N:
            yr, yi = zr[n0 : n0 + b], zi[n0 : n0 + b]
            for k in range(b):
                cr = spread(ar[n0 : n0 + b, f + k : f + k + 1], b)
                ci = spread(ai[n0 : n0 + b, f + k : f + k + 1], b)
                sr, si = spread(pr[k : k + 1], b), spread(pi[k : k + 1], b)
                yr, yi = yr - cr * sr + ci * si, yi - cr * si - ci * sr
            ahead = (yr, yi)
        lh, ll = split(jnp.concatenate([ar, ai], 1))
        prh, prl = split(pr)
        pih, pil = split(pi)

        def gap(rows):
            return [jnp.zeros((rows, 2 * N), jnp.bfloat16)] if rows else []

        def right(xr, xi):
            return jnp.concatenate(
                gap(f)
                + [jnp.concatenate([xr, xi], 1)]
                + gap(N - b)
                + [jnp.concatenate([-xi, xr], 1)]
                + gap(N - b - f),
                0,
            )

        rh, rl = right(prh, pih), right(prl, pil)
        change = d(lh, rh) + (d(ll, rh) + d(lh, rl))

        def rows(z, ch, panel, following):
            new = z - ch
            blocks = [new[:f], panel] + ([new[n0:]] if following is None else [following, new[n0 + b :]])
            return jnp.concatenate([x for x in blocks if x.shape[0]], 0)

        ar = rows(zr, change[:, :N], pr, None if ahead is None else ahead[0])
        ai = rows(zi, change[:, N:], pi, None if ahead is None else ahead[1])
    return ar, ai


def kernel(
    ham, coupling, contact, pattern, mode_weight, mode_offset, out,
    ham_in, link_in, last_in, s_ref, a_ref, b_ref, h_ref, g_ref, p_ref, q_ref, e_ref, f_ref, u_ref,
    part, schur, schur_in, join, x_ref, gee, diag, got, send, recv, esend, erecv,
):
    space, me = lax.axis_index("space"), lax.axis_index("energy")
    y, core = space // 2, space % 2
    right = y >= 2
    outer = (y == 0) | (y == 3)
    inner = jnp.logical_not(outer)
    inner_core = jnp.where(right, 1 - core, core) == 1
    nxt, prv = (y + 1) % 4, (y + 3) % 4
    other = (y * 2 + 1 - core, me)
    ahead = [(nxt * 2, me), (nxt * 2 + 1, me)]
    behind = [(prv * 2, me), (prv * 2 + 1, me)]
    pair = ((y + 1 - 2 * (y % 2)) * 2 + core, me)
    middle = ((3 - y) * 2 + core, me)
    targets = [(space, (me + d) % ENERGIES) for d in STEPS]

    def remote(src, dst, i, to):
        return pltpu.make_async_remote_copy(
            src, dst, send.at[i], recv.at[i], device_id=to, device_id_type=MESH
        )

    barrier = pltpu.get_barrier_semaphore()
    for partner in [other] + ahead + behind + targets:
        pl.semaphore_signal(barrier, inc=1, device_id=partner, device_id_type=MESH)
    pl.semaphore_wait(barrier, 8)

    send_ham = remote(ham, ham_in, 0, other)
    send_link = remote(coupling, link_in, 1, other)
    last = [remote(coupling.at[1], last_in, 2 + i, ahead[i]) for i in range(2)]
    send_ham.start()
    send_link.start()

    @pl.when(core == 1)
    def _():
        last[0].start()
        last[1].start()

    energy = -2.0 + 4.0 * (me.astype(F32) + 0.5) / ENERGIES
    eye = jnp.where(
        lax.broadcasted_iota(jnp.int32, (N, N), 0) == lax.broadcasted_iota(jnp.int32, (N, N), 1), 1.0, 0.0
    )
    zero = jnp.zeros((N, N), F32)

    def place_block(ref, i, b):
        k = jnp.where(right, 3 - b, b)
        h = get(ref, i)
        a_ref[k, 0] = energy * eye - 0.5 * (h[0] + h[0].T)
        a_ref[k, 1] = BROADENING * eye - 0.5 * (h[1] - h[1].T)

    def place_link(value, slot):
        turned = adj(value)
        put(b_ref, pick(right, turned, value), slot)
        put(h_ref, pick(right, value, turned), slot)

    def link_slot(b):
        return jnp.where(right, jnp.where(b == 3, 4, 2 - b), b)

    for i in range(2):
        place_block(ham, i, core * 2 + i)
        place_link(get(coupling, i), link_slot(core * 2 + i))
    send_ham.wait()
    for i in range(2):
        place_block(ham_in, i, (1 - core) * 2 + i)
    send_link.wait()
    for i in range(2):
        place_link(get(link_in, i), link_slot((1 - core) * 2 + i))

    @pl.when(core == 1)
    def _():
        last[0].wait_send()
        last[1].wait_send()
        last[1].wait_recv()

    @pl.when(core == 0)
    def _():
        last[0].wait_recv()

    place_link(get(last_in), jnp.where(right, 3, 4))
    lead, lead_adj = get(b_ref, 4), get(h_ref, 4)
    own = get(contact)
    gamma = mul(pick(right, lead, own), pick(right, lead_adj, adj(own)))
    weight = jnp.where(outer, 0.5, 0.0)
    put(s_ref, (a_ref[0, 0] - weight * gamma[1], a_ref[0, 1] + weight * gamma[0]))
    put(e_ref, pick(outer, (zero, zero), lead), 0)
    put(f_ref, pick(outer, (zero, zero), lead_adj), 0)
    put(u_ref, (zero, zero))

    send_schur = remote(schur.at[0], schur_in.at[0], 4, pair)
    send_middle = remote(schur.at[1], schur_in.at[1], 5, middle)
    send_green = remote(gee, x_ref, 6, pair)

    def level(k, _):
        g = inverse(get(s_ref))

        @pl.when(k < 3)
        def _():
            put(g_ref, g, k)
            p = mul(g, get(b_ref, k))
            new = sub(get(a_ref, k + 1), mul(get(h_ref, k), p))
            put(s_ref, new)

            @pl.when(k == 2)
            def _():
                put(schur, new, 0)
                send_schur.start()

            q = mul(get(h_ref, k), g, dot3)
            put(p_ref, p, k)
            put(q_ref, q, k)
            e, f = get(e_ref, k), get(f_ref, k)
            put(e_ref, mul(e, p, dot3), k + 1)
            put(f_ref, mul(q, f, dot3), k + 1)
            put(u_ref, add(get(u_ref), mul(mul(e, g, dot3), f, dot3)))

        @pl.when((k == 2) & inner_core)
        def _():
            g2 = get(g_ref, 2)
            put(part, g2, 0, 0)
            put(part, get(p_ref, 2), 0, 1)
            put(part, get(q_ref, 2), 0, 2)
            put(part, mul(g2, get(f_ref, 2), dot3), 0, 3)
            put(part, mul(get(e_ref, 2), g2, dot3), 0, 4)
            put(part, (zero, zero), 1, 0)
            put(part, (eye, zero), 1, 1)
            put(part, (eye, zero), 1, 2)
            put(part, (zero, zero), 1, 3)
            put(part, (zero, zero), 1, 4)

        @pl.when((k == 2) & jnp.logical_not(inner_core))
        def _():
            p0, p1, q0, q1 = get(p_ref, 0), get(p_ref, 1), get(q_ref, 0), get(q_ref, 1)
            w1 = add(get(g_ref, 1), mul(mul(p1, get(g_ref, 2), dot3), q1, dot3))
            l1, r1 = mul(p1, get(p_ref, 2), dot3), mul(get(q_ref, 2), q1, dot3)
            put(part, w1, 0, 0)
            put(part, l1, 0, 1)
            put(part, r1, 0, 2)
            put(part, mul(w1, get(f_ref, 1), dot3), 0, 3)
            put(part, mul(get(e_ref, 1), w1, dot3), 0, 4)
            w0 = add(get(g_ref, 0), mul(mul(p0, w1, dot3), q0, dot3))
            put(part, w0, 1, 0)
            put(part, mul(p0, l1, dot3), 1, 1)
            put(part, mul(r1, q0, dot3), 1, 2)
            put(part, mul(w0, get(f_ref, 0), dot3), 1, 3)
            put(part, mul(get(e_ref, 0), w0, dot3), 1, 4)

        @pl.when(k == 2)
        def _():
            send_schur.wait()
            put(s_ref, sub(get(schur_in, 0), get(u_ref)))

        @pl.when(k == 3)
        def _():
            e3, f3 = get(e_ref, 3), get(f_ref, 3)
            ke = mul(g, e3)
            put(schur, sub(get(schur, 0), mul(f3, ke)), 1)
            send_middle.start()
            fk = mul(f3, g, dot3)
            put(join, g, 0)
            put(join, ke, 1)
            put(join, fk, 2)
            for t in range(2):
                le, re = get(part, t, 3), get(part, t, 4)
                put(part, add(get(part, t, 0), mul(mul(le, g, dot3), re, dot3)), t, 0)
                put(part, add(get(part, t, 1), mul(le, ke, dot3)), t, 1)
                put(part, add(get(part, t, 2), mul(fk, re, dot3)), t, 2)
            send_middle.wait()
            s_ref[...] = schur_in[1]

        @pl.when(k == 4)
        def _():
            put(s_ref, sub(get(schur, 1), mul(mul(get(b_ref, 3), g), get(h_ref, 3))))

        @pl.when((k == 5) & inner)
        def _():
            put(gee, add(get(join, 0), mul(get(join, 1), mul(g, get(join, 2)))))
            send_green.start()
            put(x_ref, g)

        return 0

    lax.fori_loop(0, 6, level, 0)

    @pl.when(outer)
    def _():
        send_green.wait_recv()

    x = get(x_ref)
    copies = []
    for t in range(2):
        put(diag, add(get(part, t, 0), mul(mul(get(part, t, 1), x), get(part, t, 2))), t)
        for i, to in enumerate(targets):
            copy = pltpu.make_async_remote_copy(
                diag.at[t], got.at[i, t], esend.at[i, t], erecv.at[i, t], device_id=to, device_id_type=MESH
            )
            copy.start()
            copies.append(copy)

    @pl.when(inner)
    def _():
        send_green.wait_send()

    half = ENERGIES // 2
    shifts = [
        (jnp.where(me >= 1, 1, 99)),
        (jnp.where(me <= ENERGIES - 2, -1, 99)),
        (jnp.where(me >= half, half, -half)),
    ]
    weights = []
    for shift in shifts:
        w = jnp.float32(0.0)
        for m in range(4):
            w = w + jnp.where(mode_offset[m] == shift, mode_weight[m], 0.0)
        weights.append(w)
    mask = pattern[...].astype(F32)
    first = jnp.where(right, inner_core, jnp.logical_not(inner_core)).astype(jnp.int32)
    for t in range(2):
        for i in range(3):
            copies[3 * t + i].wait()
        slot = first if t == 0 else 1 - first
        for c in range(2):
            total = got[0, t, c] * weights[0] + got[1, t, c] * weights[1] + got[2, t, c] * weights[2]
            out[0, slot, c] = total * mask


def on_device(ham_diag, coupling, contact_left, mode_weight, mode_offset, pattern):
    blocks = [(2,), (2,), (), (), (4,), (5,), (5,), (3,), (3,), (3,), (4,), (4,), ()]
    blocks += [(2, 5), (2,), (2,), (3,), (), (), (2,), (3, 2)]
    return pl.pallas_call(
        kernel,
        out_shape=jax.ShapeDtypeStruct((1, 2) + BLOCK, F32),
        in_specs=[VM, VM, VM, VM, SM, SM],
        out_specs=VM,
        scratch_shapes=[pltpu.VMEM(b + BLOCK, F32) for b in blocks]
        + [
            pltpu.SemaphoreType.DMA((7,)),
            pltpu.SemaphoreType.DMA((7,)),
            pltpu.SemaphoreType.DMA((3, 2)),
            pltpu.SemaphoreType.DMA((3, 2)),
        ],
        compiler_params=pltpu.CompilerParams(
            collective_id=0, has_side_effects=True, vmem_limit_bytes=48 << 20
        ),
    )(ham_diag, coupling, contact_left, pattern, mode_weight, mode_offset)


def solution(mesh):
    placed = (P("space", None, None, None), P("space", None, None, None), P(), P(), P(), P())
    return jax.shard_map(
        on_device,
        mesh=mesh,
        in_specs=placed,
        out_specs=P("energy", "space", None, None, None),
        check_vma=False,
    )
```

```python
import functools

import jax
import jax.numpy as jnp
from jax import lax
from jax.experimental import pallas as pl
from jax.experimental.pallas import tpu as pltpu
from jax.sharding import PartitionSpec as P

N = 128
PANEL = 16
ENERGIES = 16
BROADENING = 0.1
F32 = jnp.float32
MESH = pl.DeviceIdType.MESH
VM = pl.BlockSpec(memory_space=pltpu.VMEM)
HB = pl.BlockSpec(memory_space=pltpu.HBM)
HIGHEST = lax.Precision.HIGHEST
BLOCK = (2, N, N)
STEPS = (1, ENERGIES - 1, ENERGIES // 2)


def split(x):
    high = x.astype(jnp.bfloat16)
    return high, (x - high.astype(F32)).astype(jnp.bfloat16)


def dot3(a, b):
    ah, al = split(a)
    bh, bl = split(b)
    d = functools.partial(jnp.dot, preferred_element_type=F32)
    return d(ah, bh) + (d(al, bh) + d(ah, bl))


def dot6(a, b):
    return jnp.dot(a, b, precision=HIGHEST, preferred_element_type=F32)


def mul(a, b, dot=dot6):
    left = jnp.concatenate([a[0], a[1]], 1)
    right = jnp.concatenate(
        [jnp.concatenate([b[0], b[1]], 1), jnp.concatenate([-b[1], b[0]], 1)], 0
    )
    out = dot(left, right)
    return out[:, :N], out[:, N:]


def add(a, b):
    return a[0] + b[0], a[1] + b[1]


def sub(a, b):
    return a[0] - b[0], a[1] - b[1]


def adj(a):
    return a[0].T, -a[1].T


def pick(cond, a, b):
    return jnp.where(cond, a[0], b[0]), jnp.where(cond, a[1], b[1])


def get(ref, *index):
    return ref[index + (0,)], ref[index + (1,)]


def put(ref, value, *index):
    ref[index + (0,)] = value[0]
    ref[index + (1,)] = value[1]


def spread(x, rows):
    return jnp.broadcast_to(x, (rows, N))


def pivot8(x, c0):
    xr, xi = x
    lane = lax.broadcasted_iota(jnp.int32, (8, N), 1)
    row = lax.broadcasted_iota(jnp.int32, (8, N), 0)
    here = (lane >= c0) & (lane < c0 + 8)
    unit = jnp.where(lane - c0 == row, 1.0, 0.0)
    zr = jnp.stack([spread(xr[:, c0 + j : c0 + j + 1], 8) for j in range(8)] + [jnp.where(here, unit, xr)])
    zi = jnp.stack([spread(xi[:, c0 + j : c0 + j + 1], 8) for j in range(8)] + [jnp.where(here, 0.0, xi)])
    qr = qi = jnp.zeros((8, N), F32)
    for k in range(8):
        dr, di = zr[0], zi[0]
        zr, zi = zr[1:], zi[1:]
        pr, pi = spread(dr[k : k + 1], 8), spread(di[k : k + 1], 8)
        inv = 1.0 / (pr * pr + pi * pi)
        at_pivot = row == k
        fr = jnp.where(at_pivot, 0.0, dr * pr + di * pi)[None]
        fi = jnp.where(at_pivot, 0.0, di * pr - dr * pi)[None]
        qr = jnp.where(at_pivot, pr * inv, qr)
        qi = jnp.where(at_pivot, -pi * inv, qi)
        shape = (8 - k, 8, N)
        ar = jnp.broadcast_to(zr[:, k : k + 1, :], shape)
        ai = jnp.broadcast_to(zi[:, k : k + 1, :], shape)
        zr = zr - (fr * ar - fi * ai) * inv[None]
        zi = zi - (fr * ai + fi * ar) * inv[None]
    return qr * zr[0] - qi * zi[0], qr * zi[0] + qi * zr[0]


def follow(x, solved, c0):
    xr, xi = x
    rows = xr.shape[0]
    lane = lax.broadcasted_iota(jnp.int32, (rows, N), 1)
    here = (lane >= c0) & (lane < c0 + 8)
    yr, yi = jnp.where(here, 0.0, xr), jnp.where(here, 0.0, xi)
    for k in range(8):
        cr, ci = spread(xr[:, c0 + k : c0 + k + 1], rows), spread(xi[:, c0 + k : c0 + k + 1], rows)
        sr, si = spread(solved[0][k : k + 1], rows), spread(solved[1][k : k + 1], rows)
        yr, yi = yr - (cr * sr - ci * si), yi - (cr * si + ci * sr)
    return yr, yi


def inverse(a):
    ar, ai = a
    b = PANEL
    lane = lax.broadcasted_iota(jnp.int32, (N, N), 1)

    def groups(first):
        return [(ar[r : r + 8], ai[r : r + 8]) for r in range(first, first + b, 8)]

    panel = groups(0)
    for f in range(0, N, b):
        n0 = f + b
        others = groups(n0) if n0 < N else []
        for g in range(b // 8):
            c0 = f + 8 * g
            solved = pivot8(panel[g], c0)
            panel = [solved if v == g else follow(x, solved, c0) for v, x in enumerate(panel)]
            others = [follow(x, solved, c0) for x in others]
        pr = jnp.concatenate([x[0] for x in panel], 0)
        pi = jnp.concatenate([x[1] for x in panel], 0)
        inside = (lane >= f) & (lane < f + b)
        zr, zi = jnp.where(inside, 0.0, ar), jnp.where(inside, 0.0, ai)

        def gap(rows):
            return [jnp.zeros((rows, 2 * N), F32)] if rows else []

        right = jnp.concatenate(
            gap(f)
            + [jnp.concatenate([pr, pi], 1)]
            + gap(N - b)
            + [jnp.concatenate([-pi, pr], 1)]
            + gap(N - b - f),
            0,
        )
        change = dot6(jnp.concatenate([ar, ai], 1), right)

        def rows(z, ch, part):
            new = z - ch
            blocks = [new[:f]] + [x[part] for x in panel + others] + [new[f + 8 * len(panel + others) :]]
            return jnp.concatenate([x for x in blocks if x.shape[0]], 0)

        ar, ai = rows(zr, change[:, :N], 0), rows(zi, change[:, N:], 1)
        panel = others
    return ar, ai


def kernel(
    ham_hbm, coupling_hbm, contact_hbm, pattern_hbm, weight_hbm, offset_hbm, out,
    ham, coupling, contact, pattern, mode_weight, mode_offset, local, ham_in, link_in, last_in, s_ref, a_ref, b_ref, h_ref, g_ref, p_ref, q_ref, e_ref, f_ref, u_ref,
    part, schur, schur_in, join, x_ref, gee, diag, got, send, recv, esend, erecv,
):
    space, me = lax.axis_index("space"), lax.axis_index("energy")
    y, core = space // 2, space % 2
    right = y >= 2
    outer = (y == 0) | (y == 3)
    inner = jnp.logical_not(outer)
    inner_core = jnp.where(right, 1 - core, core) == 1
    nxt, prv = (y + 1) % 4, (y + 3) % 4
    other = (y * 2 + 1 - core, me)
    ahead = [(nxt * 2, me), (nxt * 2 + 1, me)]
    behind = [(prv * 2, me), (prv * 2 + 1, me)]
    pair = ((y + 1 - 2 * (y % 2)) * 2 + core, me)
    middle = ((3 - y) * 2 + core, me)
    targets = [(space, (me + d) % ENERGIES) for d in STEPS]

    def remote(src, dst, i, to):
        return pltpu.make_async_remote_copy(
            src, dst, send.at[i], recv.at[i], device_id=to, device_id_type=MESH
        )

    loads = [
        pltpu.make_async_copy(src, dst, local.at[i])
        for i, (src, dst) in enumerate(
            [
                (ham_hbm, ham),
                (coupling_hbm, coupling),
                (contact_hbm, contact),
                (pattern_hbm, pattern),
                (weight_hbm, mode_weight),
                (offset_hbm, mode_offset),
            ]
        )
    ]
    for load in loads:
        load.start()
    barrier = pltpu.get_barrier_semaphore()
    for partner in [other] + ahead + behind + targets:
        pl.semaphore_signal(barrier, inc=1, device_id=partner, device_id_type=MESH)
    pl.semaphore_wait(barrier, 8)

    near = jnp.where(right, 1, 0)
    far = 1 - near
    first_block = remote(ham_hbm.at[near], ham_in.at[near], 0, other)
    first_link = remote(coupling_hbm.at[1], link_in.at[1], 1, other)
    last = [remote(coupling_hbm.at[1], last_in, 2 + i, ahead[i]) for i in range(2)]
    next_link = remote(coupling_hbm.at[0], link_in.at[0], 7, other)
    next_block = remote(ham_hbm.at[far], ham_in.at[far], 8, other)
    first_block.start()
    first_link.start()

    @pl.when(core == 1)
    def _():
        last[0].start()
        last[1].start()

    next_link.start()
    next_block.start()

    energy = -2.0 + 4.0 * (me.astype(F32) + 0.5) / ENERGIES
    eye = jnp.where(
        lax.broadcasted_iota(jnp.int32, (N, N), 0) == lax.broadcasted_iota(jnp.int32, (N, N), 1), 1.0, 0.0
    )
    zero = jnp.zeros((N, N), F32)

    def place_block(ref, i, b):
        k = jnp.where(right, 3 - b, b)
        h = get(ref, i)
        a_ref[k, 0] = energy * eye - 0.5 * (h[0] + h[0].T)
        a_ref[k, 1] = BROADENING * eye - 0.5 * (h[1] - h[1].T)

    def place_link(value, slot):
        turned = adj(value)
        put(b_ref, pick(right, turned, value), slot)
        put(h_ref, pick(right, value, turned), slot)

    def link_slot(b):
        return jnp.where(right, jnp.where(b == 3, 4, 2 - b), b)

    for load in loads[:3]:
        load.wait()
    for i in range(2):
        place_block(ham, i, core * 2 + i)
        place_link(get(coupling, i), link_slot(core * 2 + i))
    first_block.wait()
    place_block(ham_in, near, (1 - core) * 2 + near)
    first_link.wait()
    place_link(get(link_in, 1), link_slot((1 - core) * 2 + 1))
    lead, own = get(b_ref, 4), get(contact)
    lead = pick(right, lead, own)
    gamma = mul(lead, adj(lead))
    weight = jnp.where(outer, 0.5, 0.0)
    put(s_ref, (a_ref[0, 0] - weight * gamma[1], a_ref[0, 1] + weight * gamma[0]))
    put(u_ref, (zero, zero))

    def rest():
        next_link.wait()
        place_link(get(link_in, 0), link_slot((1 - core) * 2))
        next_block.wait()
        place_block(ham_in, far, (1 - core) * 2 + far)

        @pl.when(core == 1)
        def _():
            last[0].wait_send()
            last[1].wait_send()
            last[1].wait_recv()

        @pl.when(core == 0)
        def _():
            last[0].wait_recv()

        place_link(get(last_in), jnp.where(right, 3, 4))
        put(e_ref, pick(outer, (zero, zero), get(b_ref, 4)), 0)
        put(f_ref, pick(outer, (zero, zero), get(h_ref, 4)), 0)

    send_schur = remote(schur.at[0], schur_in.at[0], 4, pair)
    send_middle = remote(schur.at[1], schur_in.at[1], 5, middle)
    send_green = remote(gee, x_ref, 6, pair)

    def level(k, _):
        g = inverse(get(s_ref))

        @pl.when(k == 0)
        def _():
            rest()

        @pl.when(k < 3)
        def _():
            put(g_ref, g, k)
            p = mul(g, get(b_ref, k))
            new = sub(get(a_ref, k + 1), mul(get(h_ref, k), p))
            put(s_ref, new)

            @pl.when(k == 2)
            def _():
                put(schur, new, 0)
                send_schur.start()

            q = mul(get(h_ref, k), g, dot3)
            put(p_ref, p, k)
            put(q_ref, q, k)
            e, f = get(e_ref, k), get(f_ref, k)
            put(e_ref, mul(e, p, dot3), k + 1)
            put(f_ref, mul(q, f, dot3), k + 1)
            put(u_ref, add(get(u_ref), mul(mul(e, g, dot3), f, dot3)))

        @pl.when((k == 2) & inner_core)
        def _():
            g2 = get(g_ref, 2)
            put(part, g2, 0, 0)
            put(part, get(p_ref, 2), 0, 1)
            put(part, get(q_ref, 2), 0, 2)
            put(part, mul(g2, get(f_ref, 2), dot3), 0, 3)
            put(part, mul(get(e_ref, 2), g2, dot3), 0, 4)
            put(part, (zero, zero), 1, 0)
            put(part, (eye, zero), 1, 1)
            put(part, (eye, zero), 1, 2)
            put(part, (zero, zero), 1, 3)
            put(part, (zero, zero), 1, 4)

        @pl.when((k == 2) & jnp.logical_not(inner_core))
        def _():
            p0, p1, q0, q1 = get(p_ref, 0), get(p_ref, 1), get(q_ref, 0), get(q_ref, 1)
            w1 = add(get(g_ref, 1), mul(mul(p1, get(g_ref, 2), dot3), q1, dot3))
            l1, r1 = mul(p1, get(p_ref, 2), dot3), mul(get(q_ref, 2), q1, dot3)
            put(part, w1, 0, 0)
            put(part, l1, 0, 1)
            put(part, r1, 0, 2)
            put(part, mul(w1, get(f_ref, 1), dot3), 0, 3)
            put(part, mul(get(e_ref, 1), w1, dot3), 0, 4)
            w0 = add(get(g_ref, 0), mul(mul(p0, w1, dot3), q0, dot3))
            put(part, w0, 1, 0)
            put(part, mul(p0, l1, dot3), 1, 1)
            put(part, mul(r1, q0, dot3), 1, 2)
            put(part, mul(w0, get(f_ref, 0), dot3), 1, 3)
            put(part, mul(get(e_ref, 0), w0, dot3), 1, 4)

        @pl.when(k == 2)
        def _():
            send_schur.wait()
            put(s_ref, sub(get(schur_in, 0), get(u_ref)))

        @pl.when(k == 3)
        def _():
            e3, f3 = get(e_ref, 3), get(f_ref, 3)
            ke = mul(g, e3)
            put(schur, sub(get(schur, 0), mul(f3, ke)), 1)
            send_middle.start()
            fk = mul(f3, g, dot3)
            put(join, g, 0)
            put(join, ke, 1)
            put(join, fk, 2)
            for t in range(2):
                le, re = get(part, t, 3), get(part, t, 4)
                put(part, add(get(part, t, 0), mul(mul(le, g, dot3), re, dot3)), t, 0)
                put(part, add(get(part, t, 1), mul(le, ke, dot3)), t, 1)
                put(part, add(get(part, t, 2), mul(fk, re, dot3)), t, 2)
            send_middle.wait()
            s_ref[...] = schur_in[1]

        @pl.when(k == 4)
        def _():
            put(s_ref, sub(get(schur, 1), mul(mul(get(b_ref, 3), g), get(h_ref, 3))))

        @pl.when((k == 5) & inner)
        def _():
            put(gee, add(get(join, 0), mul(get(join, 1), mul(g, get(join, 2)))))
            send_green.start()
            put(x_ref, g)

        return 0

    lax.fori_loop(0, 6, level, 0)

    @pl.when(outer)
    def _():
        send_green.wait_recv()

    x = get(x_ref)
    copies = []
    for t in range(2):
        put(diag, add(get(part, t, 0), mul(mul(get(part, t, 1), x), get(part, t, 2))), t)
        for i, to in enumerate(targets):
            copy = pltpu.make_async_remote_copy(
                diag.at[t], got.at[i, t], esend.at[i, t], erecv.at[i, t], device_id=to, device_id_type=MESH
            )
            copy.start()
            copies.append(copy)

    @pl.when(inner)
    def _():
        send_green.wait_send()

    for load in loads[3:]:
        load.wait()
    half = ENERGIES // 2
    shifts = [
        (jnp.where(me >= 1, 1, 99)),
        (jnp.where(me <= ENERGIES - 2, -1, 99)),
        (jnp.where(me >= half, half, -half)),
    ]
    weights = []
    for shift in shifts:
        w = jnp.float32(0.0)
        for m in range(4):
            w = w + jnp.where(mode_offset[m] == shift, mode_weight[m], 0.0)
        weights.append(w)
    mask = pattern[...].astype(F32)
    first = jnp.where(right, inner_core, jnp.logical_not(inner_core)).astype(jnp.int32)
    for t in range(2):
        for i in range(3):
            copies[3 * t + i].wait()
        slot = first if t == 0 else 1 - first
        for c in range(2):
            total = got[0, t, c] * weights[0] + got[1, t, c] * weights[1] + got[2, t, c] * weights[2]
            out[0, slot, c] = total * mask


def on_device(ham_diag, coupling, contact_left, mode_weight, mode_offset, pattern):
    blocks = [(2,), (2,), (), (), (4,), (5,), (5,), (3,), (3,), (3,), (4,), (4,), ()]
    blocks += [(2, 5), (2,), (2,), (3,), (), (), (2,), (3, 2)]
    return pl.pallas_call(
        kernel,
        out_shape=jax.ShapeDtypeStruct((1, 2) + BLOCK, F32),
        in_specs=[HB] * 6,
        out_specs=VM,
        scratch_shapes=[pltpu.VMEM(b + BLOCK, F32) for b in ((2,), (2,), ())]
        + [
            pltpu.VMEM((N, N), jnp.int32),
            pltpu.SMEM((4,), F32),
            pltpu.SMEM((4,), jnp.int32),
            pltpu.SemaphoreType.DMA((6,)),
        ]
        + [pltpu.VMEM(b + BLOCK, F32) for b in blocks]
        + [
            pltpu.SemaphoreType.DMA((9,)),
            pltpu.SemaphoreType.DMA((9,)),
            pltpu.SemaphoreType.DMA((3, 2)),
            pltpu.SemaphoreType.DMA((3, 2)),
        ],
        compiler_params=pltpu.CompilerParams(
            collective_id=0, has_side_effects=True, vmem_limit_bytes=56 << 20
        ),
    )(ham_diag, coupling, contact_left, pattern, mode_weight, mode_offset)


def solution(mesh):
    placed = (P("space", None, None, None), P("space", None, None, None), P(), P(), P(), P())
    return jax.shard_map(
        on_device,
        mesh=mesh,
        in_specs=placed,
        out_specs=P("energy", "space", None, None, None),
        check_vma=False,
    )
```

```python
import functools

import jax
import jax.numpy as jnp
from jax import lax
from jax.experimental import pallas as pl
from jax.experimental.pallas import tpu as pltpu
from jax.sharding import PartitionSpec as P

N = 128
PANEL = 16
ENERGIES = 16
BROADENING = 0.1
F32 = jnp.float32
MESH = pl.DeviceIdType.MESH
VM = pl.BlockSpec(memory_space=pltpu.VMEM)
HB = pl.BlockSpec(memory_space=pltpu.HBM)
HIGHEST = lax.Precision.HIGHEST
BLOCK = (2, N, N)
STEPS = (1, ENERGIES - 1, ENERGIES // 2)


def split(x):
    high = x.astype(jnp.bfloat16)
    return high, (x - high.astype(F32)).astype(jnp.bfloat16)


def dot3(a, b):
    ah, al = split(a)
    bh, bl = split(b)
    d = functools.partial(jnp.dot, preferred_element_type=F32)
    return d(ah, bh) + (d(al, bh) + d(ah, bl))


def dot6(a, b):
    return jnp.dot(a, b, precision=HIGHEST, preferred_element_type=F32)


def mul(a, b, dot=dot6):
    left = jnp.concatenate([a[0], a[1]], 1)
    right = jnp.concatenate(
        [jnp.concatenate([b[0], b[1]], 1), jnp.concatenate([-b[1], b[0]], 1)], 0
    )
    out = dot(left, right)
    return out[:, :N], out[:, N:]


def add(a, b):
    return a[0] + b[0], a[1] + b[1]


def sub(a, b):
    return a[0] - b[0], a[1] - b[1]


def adj(a):
    return a[0].T, -a[1].T


def pick(cond, a, b):
    return jnp.where(cond, a[0], b[0]), jnp.where(cond, a[1], b[1])


def get(ref, *index):
    return ref[index + (0,)], ref[index + (1,)]


def put(ref, value, *index):
    ref[index + (0,)] = value[0]
    ref[index + (1,)] = value[1]


def spread(x, rows):
    return jnp.broadcast_to(x, (rows, N))


def pivot8(x, c0):
    xr, xi = x
    lane = lax.broadcasted_iota(jnp.int32, (8, N), 1)
    row = lax.broadcasted_iota(jnp.int32, (8, N), 0)
    here = (lane >= c0) & (lane < c0 + 8)
    unit = jnp.where(lane - c0 == row, 1.0, 0.0)
    zr = jnp.stack([spread(xr[:, c0 + j : c0 + j + 1], 8) for j in range(8)] + [jnp.where(here, unit, xr)])
    zi = jnp.stack([spread(xi[:, c0 + j : c0 + j + 1], 8) for j in range(8)] + [jnp.where(here, 0.0, xi)])
    qr = qi = jnp.zeros((8, N), F32)
    for k in range(8):
        dr, di = zr[0], zi[0]
        zr, zi = zr[1:], zi[1:]
        pr, pi = spread(dr[k : k + 1], 8), spread(di[k : k + 1], 8)
        inv = 1.0 / (pr * pr + pi * pi)
        at_pivot = row == k
        fr = jnp.where(at_pivot, 0.0, dr * pr + di * pi)[None]
        fi = jnp.where(at_pivot, 0.0, di * pr - dr * pi)[None]
        qr = jnp.where(at_pivot, pr * inv, qr)
        qi = jnp.where(at_pivot, -pi * inv, qi)
        shape = (8 - k, 8, N)
        ar = jnp.broadcast_to(zr[:, k : k + 1, :], shape)
        ai = jnp.broadcast_to(zi[:, k : k + 1, :], shape)
        zr = zr - (fr * ar - fi * ai) * inv[None]
        zi = zi - (fr * ai + fi * ar) * inv[None]
    return qr * zr[0] - qi * zi[0], qr * zi[0] + qi * zr[0]


def follow(x, solved, c0):
    xr, xi = x
    rows = xr.shape[0]
    lane = lax.broadcasted_iota(jnp.int32, (rows, N), 1)
    here = (lane >= c0) & (lane < c0 + 8)
    yr, yi = jnp.where(here, 0.0, xr), jnp.where(here, 0.0, xi)
    for k in range(8):
        cr, ci = spread(xr[:, c0 + k : c0 + k + 1], rows), spread(xi[:, c0 + k : c0 + k + 1], rows)
        sr, si = spread(solved[0][k : k + 1], rows), spread(solved[1][k : k + 1], rows)
        yr, yi = yr - (cr * sr - ci * si), yi - (cr * si + ci * sr)
    return yr, yi


def inverse(a):
    ar, ai = a
    b = PANEL
    lane = lax.broadcasted_iota(jnp.int32, (N, N), 1)

    def groups(first):
        return [(ar[r : r + 8], ai[r : r + 8]) for r in range(first, first + b, 8)]

    panel = groups(0)
    for f in range(0, N, b):
        n0 = f + b
        others = groups(n0) if n0 < N else []
        for g in range(b // 8):
            c0 = f + 8 * g
            solved = pivot8(panel[g], c0)
            panel = [solved if v == g else follow(x, solved, c0) for v, x in enumerate(panel)]
            others = [follow(x, solved, c0) for x in others]
        pr = jnp.concatenate([x[0] for x in panel], 0)
        pi = jnp.concatenate([x[1] for x in panel], 0)
        inside = (lane >= f) & (lane < f + b)
        zr, zi = jnp.where(inside, 0.0, ar), jnp.where(inside, 0.0, ai)

        def gap(rows):
            return [jnp.zeros((rows, 2 * N), F32)] if rows else []

        right = jnp.concatenate(
            gap(f)
            + [jnp.concatenate([pr, pi], 1)]
            + gap(N - b)
            + [jnp.concatenate([-pi, pr], 1)]
            + gap(N - b - f),
            0,
        )
        change = dot6(jnp.concatenate([ar, ai], 1), right)

        def rows(z, ch, part):
            new = z - ch
            blocks = [new[:f]] + [x[part] for x in panel + others] + [new[f + 8 * len(panel + others) :]]
            return jnp.concatenate([x for x in blocks if x.shape[0]], 0)

        ar, ai = rows(zr, change[:, :N], 0), rows(zi, change[:, N:], 1)
        panel = others
    return ar, ai


def kernel(
    ham_hbm, coupling_hbm, contact_hbm, pattern_hbm, weight_hbm, offset_hbm, out,
    ham, coupling, contact, pattern, mode_weight, mode_offset, local, ham_in, link_in, last_in, s_ref, a_ref, b_ref, h_ref, g_ref, p_ref, q_ref, e_ref, f_ref,
    part, schur, schur_in, join, x_ref, gee, diag, got, send, recv, esend, erecv,
):
    space, me = lax.axis_index("space"), lax.axis_index("energy")
    y, core = space // 2, space % 2
    right = y >= 2
    outer = (y == 0) | (y == 3)
    inner = jnp.logical_not(outer)
    inner_core = jnp.where(right, 1 - core, core) == 1
    nxt, prv = (y + 1) % 4, (y + 3) % 4
    other = (y * 2 + 1 - core, me)
    ahead = [(nxt * 2, me), (nxt * 2 + 1, me)]
    behind = [(prv * 2, me), (prv * 2 + 1, me)]
    pair = ((y + 1 - 2 * (y % 2)) * 2 + core, me)
    middle = ((3 - y) * 2 + core, me)
    targets = [(space, (me + d) % ENERGIES) for d in STEPS]

    def remote(src, dst, i, to):
        return pltpu.make_async_remote_copy(
            src, dst, send.at[i], recv.at[i], device_id=to, device_id_type=MESH
        )

    loads = [
        pltpu.make_async_copy(src, dst, local.at[i])
        for i, (src, dst) in enumerate(
            [
                (ham_hbm, ham),
                (coupling_hbm, coupling),
                (contact_hbm, contact),
                (pattern_hbm, pattern),
                (weight_hbm, mode_weight),
                (offset_hbm, mode_offset),
            ]
        )
    ]
    for load in loads:
        load.start()
    barrier = pltpu.get_barrier_semaphore()
    for partner in [other] + ahead + behind + targets:
        pl.semaphore_signal(barrier, inc=1, device_id=partner, device_id_type=MESH)
    pl.semaphore_wait(barrier, 8)

    near = jnp.where(right, 1, 0)
    far = 1 - near
    first_block = remote(ham_hbm.at[near], ham_in.at[near], 0, other)
    first_link = remote(coupling_hbm.at[1], link_in.at[1], 1, other)
    last = [remote(coupling_hbm.at[1], last_in, 2 + i, ahead[i]) for i in range(2)]
    next_link = remote(coupling_hbm.at[0], link_in.at[0], 7, other)
    next_block = remote(ham_hbm.at[far], ham_in.at[far], 8, other)
    first_block.start()
    first_link.start()

    @pl.when(core == 1)
    def _():
        last[0].start()
        last[1].start()

    next_link.start()
    next_block.start()

    energy = -2.0 + 4.0 * (me.astype(F32) + 0.5) / ENERGIES
    eye = jnp.where(
        lax.broadcasted_iota(jnp.int32, (N, N), 0) == lax.broadcasted_iota(jnp.int32, (N, N), 1), 1.0, 0.0
    )
    zero = jnp.zeros((N, N), F32)

    def place_block(ref, i, b):
        k = jnp.where(right, 3 - b, b)
        h = get(ref, i)
        a_ref[k, 0] = energy * eye - 0.5 * (h[0] + h[0].T)
        a_ref[k, 1] = BROADENING * eye - 0.5 * (h[1] - h[1].T)

    def place_link(value, slot):
        turned = adj(value)
        put(b_ref, pick(right, turned, value), slot)
        put(h_ref, pick(right, value, turned), slot)

    def link_slot(b):
        return jnp.where(right, jnp.where(b == 3, 4, 2 - b), b)

    for load in loads[:3]:
        load.wait()
    for i in range(2):
        place_block(ham, i, core * 2 + i)
        place_link(get(coupling, i), link_slot(core * 2 + i))
    first_block.wait()
    place_block(ham_in, near, (1 - core) * 2 + near)
    first_link.wait()
    place_link(get(link_in, 1), link_slot((1 - core) * 2 + 1))
    lead, own = get(b_ref, 4), get(contact)
    lead = pick(right, lead, own)
    gamma = mul(lead, adj(lead))
    weight = jnp.where(outer, 0.5, 0.0)
    put(s_ref, (a_ref[0, 0] - weight * gamma[1], a_ref[0, 1] + weight * gamma[0]))

    def rest():
        next_link.wait()
        place_link(get(link_in, 0), link_slot((1 - core) * 2))
        next_block.wait()
        place_block(ham_in, far, (1 - core) * 2 + far)

        @pl.when(core == 1)
        def _():
            last[0].wait_send()
            last[1].wait_send()
            last[1].wait_recv()

        @pl.when(core == 0)
        def _():
            last[0].wait_recv()

        place_link(get(last_in), jnp.where(right, 3, 4))
        put(e_ref, pick(outer, (zero, zero), get(b_ref, 4)), 0)
        put(f_ref, pick(outer, (zero, zero), get(h_ref, 4)), 0)

    send_schur = remote(schur.at[0], schur_in.at[0], 4, pair)
    send_middle = remote(schur.at[1], schur_in.at[1], 5, middle)
    send_green = remote(gee, x_ref, 6, pair)

    def level(k, _):
        g = inverse(get(s_ref))

        @pl.when(k == 0)
        def _():
            rest()

        @pl.when(k < 3)
        def _():
            put(g_ref, g, k)
            p = mul(g, get(b_ref, k))
            new = sub(get(a_ref, k + 1), mul(get(h_ref, k), p))
            put(s_ref, new)

            @pl.when(k == 2)
            def _():
                put(schur, new, 0)
                send_schur.start()

            put(p_ref, p, k)

        @pl.when(k == 2)
        def _():
            u = (zero, zero)
            for j in range(3):
                gj = get(g_ref, j)
                q = mul(get(h_ref, j), gj, dot3)
                put(q_ref, q, j)
                e, f = get(e_ref, j), get(f_ref, j)
                put(e_ref, mul(e, get(p_ref, j), dot3), j + 1)
                put(f_ref, mul(q, f, dot3), j + 1)
                u = add(u, mul(mul(e, gj, dot3), f, dot3))
            send_schur.wait()
            put(s_ref, sub(get(schur_in, 0), u))

        @pl.when(k == 3)
        def _():
            e3, f3 = get(e_ref, 3), get(f_ref, 3)
            ke = mul(g, e3)
            put(schur, sub(get(schur, 0), mul(f3, ke)), 1)
            send_middle.start()
            fk = mul(f3, g, dot3)
            put(join, g, 0)
            put(join, ke, 1)
            put(join, fk, 2)

        @pl.when((k == 3) & inner_core)
        def _():
            g2 = get(g_ref, 2)
            put(part, g2, 0, 0)
            put(part, get(p_ref, 2), 0, 1)
            put(part, get(q_ref, 2), 0, 2)
            put(part, mul(g2, get(f_ref, 2), dot3), 0, 3)
            put(part, mul(get(e_ref, 2), g2, dot3), 0, 4)
            put(part, (zero, zero), 1, 0)
            put(part, (eye, zero), 1, 1)
            put(part, (eye, zero), 1, 2)
            put(part, (zero, zero), 1, 3)
            put(part, (zero, zero), 1, 4)

        @pl.when((k == 3) & jnp.logical_not(inner_core))
        def _():
            p0, p1, q0, q1 = get(p_ref, 0), get(p_ref, 1), get(q_ref, 0), get(q_ref, 1)
            w1 = add(get(g_ref, 1), mul(mul(p1, get(g_ref, 2), dot3), q1, dot3))
            l1, r1 = mul(p1, get(p_ref, 2), dot3), mul(get(q_ref, 2), q1, dot3)
            put(part, w1, 0, 0)
            put(part, l1, 0, 1)
            put(part, r1, 0, 2)
            put(part, mul(w1, get(f_ref, 1), dot3), 0, 3)
            put(part, mul(get(e_ref, 1), w1, dot3), 0, 4)
            w0 = add(get(g_ref, 0), mul(mul(p0, w1, dot3), q0, dot3))
            put(part, w0, 1, 0)
            put(part, mul(p0, l1, dot3), 1, 1)
            put(part, mul(r1, q0, dot3), 1, 2)
            put(part, mul(w0, get(f_ref, 0), dot3), 1, 3)
            put(part, mul(get(e_ref, 0), w0, dot3), 1, 4)

        @pl.when(k == 3)
        def _():
            send_middle.wait()
            s_ref[...] = schur_in[1]

        @pl.when(k == 4)
        def _():
            put(s_ref, sub(get(schur, 1), mul(mul(get(b_ref, 3), g), get(h_ref, 3))))

        @pl.when((k == 5) & inner)
        def _():
            put(gee, add(get(join, 0), mul(get(join, 1), mul(g, get(join, 2)))))
            send_green.start()
            put(x_ref, g)
            kk, ke, fk = get(join, 0), get(join, 1), get(join, 2)
            for t in range(2):
                le, re = get(part, t, 3), get(part, t, 4)
                put(part, add(get(part, t, 0), mul(mul(le, kk, dot3), re, dot3)), t, 0)
                put(part, add(get(part, t, 1), mul(le, ke, dot3)), t, 1)
                put(part, add(get(part, t, 2), mul(fk, re, dot3)), t, 2)

        return 0

    lax.fori_loop(0, 6, level, 0)

    @pl.when(outer)
    def _():
        send_green.wait_recv()

    x = get(x_ref)
    copies = []
    for t in range(2):
        put(diag, add(get(part, t, 0), mul(mul(get(part, t, 1), x), get(part, t, 2))), t)
        for i, to in enumerate(targets):
            copy = pltpu.make_async_remote_copy(
                diag.at[t], got.at[i, t], esend.at[i, t], erecv.at[i, t], device_id=to, device_id_type=MESH
            )
            copy.start()
            copies.append(copy)

    @pl.when(inner)
    def _():
        send_green.wait_send()

    for load in loads[3:]:
        load.wait()
    half = ENERGIES // 2
    shifts = [
        (jnp.where(me >= 1, 1, 99)),
        (jnp.where(me <= ENERGIES - 2, -1, 99)),
        (jnp.where(me >= half, half, -half)),
    ]
    weights = []
    for shift in shifts:
        w = jnp.float32(0.0)
        for m in range(4):
            w = w + jnp.where(mode_offset[m] == shift, mode_weight[m], 0.0)
        weights.append(w)
    mask = pattern[...].astype(F32)
    first = jnp.where(right, inner_core, jnp.logical_not(inner_core)).astype(jnp.int32)
    for t in range(2):
        for i in range(3):
            copies[3 * t + i].wait()
        slot = first if t == 0 else 1 - first
        for c in range(2):
            total = got[0, t, c] * weights[0] + got[1, t, c] * weights[1] + got[2, t, c] * weights[2]
            out[0, slot, c] = total * mask


def on_device(ham_diag, coupling, contact_left, mode_weight, mode_offset, pattern):
    blocks = [(2,), (2,), (), (), (4,), (5,), (5,), (3,), (3,), (3,), (4,), (4,)]
    blocks += [(2, 5), (2,), (2,), (3,), (), (), (2,), (3, 2)]
    return pl.pallas_call(
        kernel,
        out_shape=jax.ShapeDtypeStruct((1, 2) + BLOCK, F32),
        in_specs=[HB] * 6,
        out_specs=VM,
        scratch_shapes=[pltpu.VMEM(b + BLOCK, F32) for b in ((2,), (2,), ())]
        + [
            pltpu.VMEM((N, N), jnp.int32),
            pltpu.SMEM((4,), F32),
            pltpu.SMEM((4,), jnp.int32),
            pltpu.SemaphoreType.DMA((6,)),
        ]
        + [pltpu.VMEM(b + BLOCK, F32) for b in blocks]
        + [
            pltpu.SemaphoreType.DMA((9,)),
            pltpu.SemaphoreType.DMA((9,)),
            pltpu.SemaphoreType.DMA((3, 2)),
            pltpu.SemaphoreType.DMA((3, 2)),
        ],
        compiler_params=pltpu.CompilerParams(
            collective_id=0, has_side_effects=True, vmem_limit_bytes=56 << 20
        ),
    )(ham_diag, coupling, contact_left, pattern, mode_weight, mode_offset)


def solution(mesh):
    placed = (P("space", None, None, None), P("space", None, None, None), P(), P(), P(), P())
    return jax.shard_map(
        on_device,
        mesh=mesh,
        in_specs=placed,
        out_specs=P("energy", "space", None, None, None),
        check_vma=False,
    )
```

```python
import functools

import jax
import jax.numpy as jnp
from jax import lax
from jax.experimental import pallas as pl
from jax.experimental.pallas import tpu as pltpu
from jax.sharding import PartitionSpec as P

N = 128
PANEL = 16
ENERGIES = 16
BROADENING = 0.1
F32 = jnp.float32
MESH = pl.DeviceIdType.MESH
VM = pl.BlockSpec(memory_space=pltpu.VMEM)
HB = pl.BlockSpec(memory_space=pltpu.HBM)
HIGHEST = lax.Precision.HIGHEST
BLOCK = (2, N, N)
STEPS = (1, ENERGIES - 1, ENERGIES // 2)


def split(x):
    high = x.astype(jnp.bfloat16)
    return high, (x - high.astype(F32)).astype(jnp.bfloat16)


def dot3(a, b):
    ah, al = split(a)
    bh, bl = split(b)
    d = functools.partial(jnp.dot, preferred_element_type=F32)
    return d(ah, bh) + (d(al, bh) + d(ah, bl))


def dot6(a, b):
    return jnp.dot(a, b, precision=HIGHEST, preferred_element_type=F32)


def mul(a, b, dot=dot6):
    left = jnp.concatenate([a[0], a[1]], 1)
    right = jnp.concatenate(
        [jnp.concatenate([b[0], b[1]], 1), jnp.concatenate([-b[1], b[0]], 1)], 0
    )
    out = dot(left, right)
    return out[:, :N], out[:, N:]


def add(a, b):
    return a[0] + b[0], a[1] + b[1]


def sub(a, b):
    return a[0] - b[0], a[1] - b[1]


def adj(a):
    return a[0].T, -a[1].T


def pick(cond, a, b):
    return jnp.where(cond, a[0], b[0]), jnp.where(cond, a[1], b[1])


def get(ref, *index):
    return ref[index + (0,)], ref[index + (1,)]


def put(ref, value, *index):
    ref[index + (0,)] = value[0]
    ref[index + (1,)] = value[1]


def spread(x, rows):
    return jnp.broadcast_to(x, (rows, N))


def pivot8(x, c0):
    xr, xi = x
    lane = lax.broadcasted_iota(jnp.int32, (8, N), 1)
    row = lax.broadcasted_iota(jnp.int32, (8, N), 0)
    here = (lane >= c0) & (lane < c0 + 8)
    unit = jnp.where(lane - c0 == row, 1.0, 0.0)
    zr = jnp.stack([spread(xr[:, c0 + j : c0 + j + 1], 8) for j in range(8)] + [jnp.where(here, unit, xr)])
    zi = jnp.stack([spread(xi[:, c0 + j : c0 + j + 1], 8) for j in range(8)] + [jnp.where(here, 0.0, xi)])
    qr = qi = jnp.zeros((8, N), F32)
    for k in range(8):
        dr, di = zr[0], zi[0]
        zr, zi = zr[1:], zi[1:]
        pr, pi = spread(dr[k : k + 1], 8), spread(di[k : k + 1], 8)
        inv = 1.0 / (pr * pr + pi * pi)
        at_pivot = row == k
        fr = jnp.where(at_pivot, 0.0, dr * pr + di * pi)[None]
        fi = jnp.where(at_pivot, 0.0, di * pr - dr * pi)[None]
        qr = jnp.where(at_pivot, pr * inv, qr)
        qi = jnp.where(at_pivot, -pi * inv, qi)
        shape = (8 - k, 8, N)
        ar = jnp.broadcast_to(zr[:, k : k + 1, :], shape)
        ai = jnp.broadcast_to(zi[:, k : k + 1, :], shape)
        zr = zr - (fr * ar - fi * ai) * inv[None]
        zi = zi - (fr * ai + fi * ar) * inv[None]
    return qr * zr[0] - qi * zi[0], qr * zi[0] + qi * zr[0]


def follow(x, solved, c0):
    xr, xi = x
    rows = xr.shape[0]
    lane = lax.broadcasted_iota(jnp.int32, (rows, N), 1)
    here = (lane >= c0) & (lane < c0 + 8)
    yr, yi = jnp.where(here, 0.0, xr), jnp.where(here, 0.0, xi)
    for k in range(8):
        cr, ci = spread(xr[:, c0 + k : c0 + k + 1], rows), spread(xi[:, c0 + k : c0 + k + 1], rows)
        sr, si = spread(solved[0][k : k + 1], rows), spread(solved[1][k : k + 1], rows)
        yr, yi = yr - (cr * sr - ci * si), yi - (cr * si + ci * sr)
    return yr, yi


def inverse(a):
    ar, ai = a
    b = PANEL
    lane = lax.broadcasted_iota(jnp.int32, (N, N), 1)

    def groups(first):
        return [(ar[r : r + 8], ai[r : r + 8]) for r in range(first, first + b, 8)]

    panel = groups(0)
    for f in range(0, N, b):
        n0 = f + b
        others = groups(n0) if n0 < N else []
        for g in range(b // 8):
            c0 = f + 8 * g
            solved = pivot8(panel[g], c0)
            panel = [solved if v == g else follow(x, solved, c0) for v, x in enumerate(panel)]
            others = [follow(x, solved, c0) for x in others]
        pr = jnp.concatenate([x[0] for x in panel], 0)
        pi = jnp.concatenate([x[1] for x in panel], 0)
        inside = (lane >= f) & (lane < f + b)
        zr, zi = jnp.where(inside, 0.0, ar), jnp.where(inside, 0.0, ai)

        def gap(rows):
            return [jnp.zeros((rows, 2 * N), F32)] if rows else []

        right = jnp.concatenate(
            gap(f)
            + [jnp.concatenate([pr, pi], 1)]
            + gap(N - b)
            + [jnp.concatenate([-pi, pr], 1)]
            + gap(N - b - f),
            0,
        )
        change = dot6(jnp.concatenate([ar, ai], 1), right)

        def rows(z, ch, part):
            new = z - ch
            blocks = [new[:f]] + [x[part] for x in panel + others] + [new[f + 8 * len(panel + others) :]]
            return jnp.concatenate([x for x in blocks if x.shape[0]], 0)

        ar, ai = rows(zr, change[:, :N], 0), rows(zi, change[:, N:], 1)
        panel = others
    return ar, ai


def kernel(
    ham_hbm, coupling_hbm, contact_hbm, pattern_hbm, weight_hbm, offset_hbm, out,
    ham, coupling, contact, pattern, mode_weight, mode_offset, local, ham_in, link_in, last_in, s_ref, a_ref, b_ref, h_ref, g_ref, p_ref, q_ref, e_ref, f_ref,
    part, schur, schur_in, join, x_ref, gee, diag, got, send, recv, esend, erecv,
):
    space, me = lax.axis_index("space"), lax.axis_index("energy")
    y, core = space // 2, space % 2
    right = y >= 2
    outer = (y == 0) | (y == 3)
    inner = jnp.logical_not(outer)
    inner_core = jnp.where(right, 1 - core, core) == 1
    nxt, prv = (y + 1) % 4, (y + 3) % 4
    other = (y * 2 + 1 - core, me)
    ahead = [(nxt * 2, me), (nxt * 2 + 1, me)]
    behind = [(prv * 2, me), (prv * 2 + 1, me)]
    pair = ((y + 1 - 2 * (y % 2)) * 2 + core, me)
    middle = ((3 - y) * 2 + core, me)
    targets = [(space, (me + d) % ENERGIES) for d in STEPS]

    def remote(src, dst, i, to):
        return pltpu.make_async_remote_copy(
            src, dst, send.at[i], recv.at[i], device_id=to, device_id_type=MESH
        )

    loads = [
        pltpu.make_async_copy(src, dst, local.at[i])
        for i, (src, dst) in enumerate(
            [
                (ham_hbm, ham),
                (coupling_hbm, coupling),
                (contact_hbm, contact),
                (pattern_hbm, pattern),
                (weight_hbm, mode_weight),
                (offset_hbm, mode_offset),
            ]
        )
    ]
    for load in loads:
        load.start()
    barrier = pltpu.get_barrier_semaphore()
    for partner in [other] + ahead + behind + targets:
        pl.semaphore_signal(barrier, inc=1, device_id=partner, device_id_type=MESH)
    pl.semaphore_wait(barrier, 8)

    near = jnp.where(right, 1, 0)
    far = 1 - near
    first_block = remote(ham_hbm.at[near], ham_in.at[near], 0, other)
    first_link = remote(coupling_hbm.at[1], link_in.at[1], 1, other)
    last = [remote(coupling_hbm.at[1], last_in, 2 + i, ahead[i]) for i in range(2)]
    next_link = remote(coupling_hbm.at[0], link_in.at[0], 7, other)
    next_block = remote(ham_hbm.at[far], ham_in.at[far], 8, other)
    first_block.start()
    first_link.start()

    @pl.when(core == 1)
    def _():
        last[0].start()
        last[1].start()

    next_link.start()
    next_block.start()

    energy = -2.0 + 4.0 * (me.astype(F32) + 0.5) / ENERGIES
    eye = jnp.where(
        lax.broadcasted_iota(jnp.int32, (N, N), 0) == lax.broadcasted_iota(jnp.int32, (N, N), 1), 1.0, 0.0
    )
    zero = jnp.zeros((N, N), F32)

    def place_block(ref, i, b):
        k = jnp.where(right, 3 - b, b)
        h = get(ref, i)
        a_ref[k, 0] = energy * eye - 0.5 * (h[0] + h[0].T)
        a_ref[k, 1] = BROADENING * eye - 0.5 * (h[1] - h[1].T)

    def place_link(value, slot):
        turned = adj(value)
        put(b_ref, pick(right, turned, value), slot)
        put(h_ref, pick(right, value, turned), slot)

    def link_slot(b):
        return jnp.where(right, jnp.where(b == 3, 4, 2 - b), b)

    for load in loads[:3]:
        load.wait()
    for i in range(2):
        place_block(ham, i, core * 2 + i)
        place_link(get(coupling, i), link_slot(core * 2 + i))
    first_block.wait()
    place_block(ham_in, near, (1 - core) * 2 + near)
    first_link.wait()
    place_link(get(link_in, 1), link_slot((1 - core) * 2 + 1))
    lead, own = get(b_ref, 4), get(contact)
    lead = pick(right, lead, own)
    gamma = mul(lead, adj(lead))
    weight = jnp.where(outer, 0.5, 0.0)
    put(s_ref, (a_ref[0, 0] - weight * gamma[1], a_ref[0, 1] + weight * gamma[0]))

    def rest():
        next_link.wait()
        place_link(get(link_in, 0), link_slot((1 - core) * 2))
        next_block.wait()
        place_block(ham_in, far, (1 - core) * 2 + far)

        @pl.when(core == 1)
        def _():
            last[0].wait_send()
            last[1].wait_send()
            last[1].wait_recv()

        @pl.when(core == 0)
        def _():
            last[0].wait_recv()

        place_link(get(last_in), jnp.where(right, 3, 4))
        put(e_ref, pick(outer, (zero, zero), get(b_ref, 4)), 0)
        put(f_ref, pick(outer, (zero, zero), get(h_ref, 4)), 0)

    send_schur = remote(schur.at[0], schur_in.at[0], 4, pair)
    send_middle = remote(schur.at[1], schur_in.at[1], 5, middle)
    send_green = remote(gee, x_ref, 6, pair)

    def level(k, _):
        g = inverse(get(s_ref))

        @pl.when(k == 0)
        def _():
            rest()

        @pl.when(k < 3)
        def _():
            put(g_ref, g, k)
            p = mul(g, get(b_ref, k))
            new = sub(get(a_ref, k + 1), mul(get(h_ref, k), p))
            put(s_ref, new)

            @pl.when(k == 2)
            def _():
                put(schur, new, 0)
                send_schur.start()

            put(p_ref, p, k)

        @pl.when(k == 2)
        def _():
            u = (zero, zero)
            for j in range(3):
                gj = get(g_ref, j)
                q = mul(get(h_ref, j), gj, dot3)
                put(q_ref, q, j)
                e, f = get(e_ref, j), get(f_ref, j)
                put(e_ref, mul(e, get(p_ref, j), dot3), j + 1)
                put(f_ref, mul(q, f, dot3), j + 1)
                u = add(u, mul(mul(e, gj, dot3), f, dot3))
            send_schur.wait()
            put(s_ref, sub(get(schur_in, 0), u))

        @pl.when(k == 3)
        def _():
            e3, f3 = get(e_ref, 3), get(f_ref, 3)
            ke = mul(g, e3)
            put(schur, sub(get(schur, 0), mul(f3, ke)), 1)
            send_middle.start()
            fk = mul(f3, g, dot3)
            put(join, g, 0)
            put(join, ke, 1)
            put(join, fk, 2)

        @pl.when((k == 3) & inner_core)
        def _():
            g2 = get(g_ref, 2)
            put(part, g2, 0, 0)
            put(part, get(p_ref, 2), 0, 1)
            put(part, get(q_ref, 2), 0, 2)
            put(part, mul(g2, get(f_ref, 2), dot3), 0, 3)
            put(part, mul(get(e_ref, 2), g2, dot3), 0, 4)
            put(part, (zero, zero), 1, 0)
            put(part, (eye, zero), 1, 1)
            put(part, (eye, zero), 1, 2)
            put(part, (zero, zero), 1, 3)
            put(part, (zero, zero), 1, 4)

        @pl.when((k == 3) & jnp.logical_not(inner_core))
        def _():
            p0, p1, q0, q1 = get(p_ref, 0), get(p_ref, 1), get(q_ref, 0), get(q_ref, 1)
            w1 = add(get(g_ref, 1), mul(mul(p1, get(g_ref, 2), dot3), q1, dot3))
            l1, r1 = mul(p1, get(p_ref, 2), dot3), mul(get(q_ref, 2), q1, dot3)
            put(part, w1, 0, 0)
            put(part, l1, 0, 1)
            put(part, r1, 0, 2)
            put(part, mul(w1, get(f_ref, 1), dot3), 0, 3)
            put(part, mul(get(e_ref, 1), w1, dot3), 0, 4)
            w0 = add(get(g_ref, 0), mul(mul(p0, w1, dot3), q0, dot3))
            put(part, w0, 1, 0)
            put(part, mul(p0, l1, dot3), 1, 1)
            put(part, mul(r1, q0, dot3), 1, 2)
            put(part, mul(w0, get(f_ref, 0), dot3), 1, 3)
            put(part, mul(get(e_ref, 0), w0, dot3), 1, 4)

        @pl.when(k == 3)
        def _():
            send_middle.wait()
            s_ref[...] = schur_in[1]

        @pl.when(k == 4)
        def _():
            put(s_ref, sub(get(schur, 1), mul(mul(get(b_ref, 3), g), get(h_ref, 3))))

        @pl.when((k == 5) & inner)
        def _():
            put(gee, add(get(join, 0), mul(get(join, 1), mul(g, get(join, 2), dot3), dot3)))
            send_green.start()
            put(x_ref, g)
            kk, ke, fk = get(join, 0), get(join, 1), get(join, 2)
            for t in range(2):
                le, re = get(part, t, 3), get(part, t, 4)
                put(part, add(get(part, t, 0), mul(mul(le, kk, dot3), re, dot3)), t, 0)
                put(part, add(get(part, t, 1), mul(le, ke, dot3)), t, 1)
                put(part, add(get(part, t, 2), mul(fk, re, dot3)), t, 2)

        return 0

    lax.fori_loop(0, 6, level, 0)

    @pl.when(outer)
    def _():
        send_green.wait_recv()

    x = get(x_ref)
    copies = []
    for t in range(2):
        put(diag, add(get(part, t, 0), mul(mul(get(part, t, 1), x, dot3), get(part, t, 2), dot3)), t)
        for i, to in enumerate(targets):
            copy = pltpu.make_async_remote_copy(
                diag.at[t], got.at[i, t], esend.at[i, t], erecv.at[i, t], device_id=to, device_id_type=MESH
            )
            copy.start()
            copies.append(copy)

    @pl.when(inner)
    def _():
        send_green.wait_send()

    for load in loads[3:]:
        load.wait()
    half = ENERGIES // 2
    shifts = [
        (jnp.where(me >= 1, 1, 99)),
        (jnp.where(me <= ENERGIES - 2, -1, 99)),
        (jnp.where(me >= half, half, -half)),
    ]
    weights = []
    for shift in shifts:
        w = jnp.float32(0.0)
        for m in range(4):
            w = w + jnp.where(mode_offset[m] == shift, mode_weight[m], 0.0)
        weights.append(w)
    mask = pattern[...].astype(F32)
    first = jnp.where(right, inner_core, jnp.logical_not(inner_core)).astype(jnp.int32)
    for t in range(2):
        for i in range(3):
            copies[3 * t + i].wait()
        slot = first if t == 0 else 1 - first
        for c in range(2):
            total = got[0, t, c] * weights[0] + got[1, t, c] * weights[1] + got[2, t, c] * weights[2]
            out[0, slot, c] = total * mask


def on_device(ham_diag, coupling, contact_left, mode_weight, mode_offset, pattern):
    blocks = [(2,), (2,), (), (), (4,), (5,), (5,), (3,), (3,), (3,), (4,), (4,)]
    blocks += [(2, 5), (2,), (2,), (3,), (), (), (2,), (3, 2)]
    return pl.pallas_call(
        kernel,
        out_shape=jax.ShapeDtypeStruct((1, 2) + BLOCK, F32),
        in_specs=[HB] * 6,
        out_specs=VM,
        scratch_shapes=[pltpu.VMEM(b + BLOCK, F32) for b in ((2,), (2,), ())]
        + [
            pltpu.VMEM((N, N), jnp.int32),
            pltpu.SMEM((4,), F32),
            pltpu.SMEM((4,), jnp.int32),
            pltpu.SemaphoreType.DMA((6,)),
        ]
        + [pltpu.VMEM(b + BLOCK, F32) for b in blocks]
        + [
            pltpu.SemaphoreType.DMA((9,)),
            pltpu.SemaphoreType.DMA((9,)),
            pltpu.SemaphoreType.DMA((3, 2)),
            pltpu.SemaphoreType.DMA((3, 2)),
        ],
        compiler_params=pltpu.CompilerParams(
            collective_id=0, has_side_effects=True, vmem_limit_bytes=56 << 20
        ),
    )(ham_diag, coupling, contact_left, pattern, mode_weight, mode_offset)


def solution(mesh):
    placed = (P("space", None, None, None), P("space", None, None, None), P(), P(), P(), P())
    return jax.shard_map(
        on_device,
        mesh=mesh,
        in_specs=placed,
        out_specs=P("energy", "space", None, None, None),
        check_vma=False,
    )
```
